32 devices in a mesh: dp: 8 (over y, x, core), fsdp: 4 (over z).
Axes of the slice: x: 2, y: 2, z: 4, core: 2. Of those that a mesh axis runs over, the one named last changes fastest.
Arguments:
- tokens: bfloat16 [2, 32, 128, 768], P(None, ('dp', 'fsdp')), may hold values from -6 to 6
- lengths: int32 [2, 32], P(None, ('dp', 'fsdp')), may hold values from 32 to 128, as said below
- routes: int32 [2, 2, 32, 128, 2], P(None, None, ('dp', 'fsdp')), may hold values from 0 to 7, all different within a row; in each aligned block of 128 rows (0 to 127, 128 to 255, ..., all dimensions but the last counted through in order) at most 36 rows name the same one
- cotangent: bfloat16 [2, 32, 128, 768], P(None, ('dp', 'fsdp')), may hold values from -6 to 6
- attn_gain: bfloat16 [2, 768], P(None, ('dp', 'fsdp')), may hold values from 0.5 to 1.5
- qkv_weight: bfloat16 [2, 768, 2304], P(None, ('dp', 'fsdp')), may hold values from -0.21875 to 0.21875
- out_weight: bfloat16 [2, 768, 768], P(None, ('dp', 'fsdp')), may hold values from -0.875 to 0.875
- ffn_gain: bfloat16 [2, 768], P(None, ('dp', 'fsdp')), may hold values from 0.5 to 1.5
- router_weight: bfloat16 [2, 768, 8], P(None, ('dp', 'fsdp')), may hold values from -0.15625 to 0.15625
- shared_gate: bfloat16 [2, 768, 2048], P(None, ('dp', 'fsdp')), may hold values from -0.21875 to 0.21875
- shared_up: bfloat16 [2, 768, 2048], P(None, ('dp', 'fsdp')), may hold values from -0.21875 to 0.21875
- shared_down: bfloat16 [2, 2048, 768], P(None, ('dp', 'fsdp')), may hold values from -0.125 to 0.125
- expert_gate: bfloat16 [2, 8, 768, 2048], P(None, 'dp', None, 'fsdp'), may hold values from -0.21875 to 0.21875
- expert_up: bfloat16 [2, 8, 768, 2048], P(None, 'dp', None, 'fsdp'), may hold values from -0.21875 to 0.21875
- expert_down: bfloat16 [2, 8, 2048, 768], P(None, 'dp', 'fsdp'), may hold values from -0.125 to 0.125
Outputs:
- output: float32 [2, 32, 128, 768], P(None, ('dp', 'fsdp'))
- input_grad: float32 [2, 32, 128, 768], P(None, ('dp', 'fsdp'))
- grad_attn_gain: float32 [2, 768], P(None, ('dp', 'fsdp'))
- grad_qkv_weight: float32 [2, 768, 2304], P(None, ('dp', 'fsdp'))
- grad_out_weight: float32 [2, 768, 768], P(None, ('dp', 'fsdp'))
- grad_ffn_gain: float32 [2, 768], P(None, ('dp', 'fsdp'))
- grad_router_weight: float32 [2, 768, 8], P(None, ('dp', 'fsdp'))
- grad_shared_gate: float32 [2, 768, 2048], P(None, ('dp', 'fsdp'))
- grad_shared_up: float32 [2, 768, 2048], P(None, ('dp', 'fsdp'))
- grad_shared_down: float32 [2, 2048, 768], P(None, ('dp', 'fsdp'))
- grad_expert_gate: float32 [2, 8, 768, 2048], P(None, 'dp', None, 'fsdp')
- grad_expert_up: float32 [2, 8, 768, 2048], P(None, 'dp', None, 'fsdp')
- grad_expert_down: float32 [2, 8, 2048, 768], P(None, 'dp', 'fsdp')
The draws below stay inside these ranges and needn't reach their ends.
Inputs may be any that keep to these rules, and one draw needn't show every extreme that they name: Each slot holds one sequence from its first position on, lengths[m, s] tokens long, the rest padding; in every micro-batch some slot is full. `routes`: each token names two different experts; within the 128 rows of one slot of one layer no expert is named more than 36 times, and in some slots one expert is named exactly 36 times.
All inputs are finite; a program needn't handle non-finite values.
Results may differ from the reference program's by a relative error of at most 0.023.
Values may be sent and summed in bfloat16 or wider, within the bound.
No kernel may reach another device: no remote copies, remote signals or barrier semaphores. Data moves between devices by JAX's collectives and lax.ppermute only.
A program may use at most 384 MiB of HBM per device.

```python
import math
from functools import partial
import jax
import jax.numpy as jnp
import numpy as np
from jax import lax

D = 768
HEADS = 12
HDIM = 64
FF = 2048
LAYERS = 2
MICRO = 2
SLOT = 128
EXPERTS = 8
SEQS = 32
CAP = 36


def draw_lengths(key, part):
    key = jax.random.fold_in(key, 11)
    first_key, second_key = jax.random.split(key)
    drawn = jax.random.randint(first_key, (MICRO, SEQS), SLOT // 4, SLOT + 1)
    chosen = jax.random.randint(second_key, (MICRO, 1), 0, SEQS)
    filled = jnp.arange(SEQS)[None, :] == chosen
    return jnp.where(filled, SLOT, drawn).astype(jnp.int32)


def level_of(stream_key, extent, cuts, smallest, high):
    def one(dim, blocks):
        draws = jax.random.uniform(jax.random.fold_in(jax.random.fold_in(stream_key, 6), dim), (blocks,), jnp.float32, smallest / len(cuts), high / len(cuts))
        return jnp.repeat(jnp.exp(draws), extent[dim] // blocks).reshape((-1,) + (1,) * (len(extent) - dim - 1))

    factor_of = one(*cuts[0])
    for cut in cuts[1:]:
        factor_of = factor_of * one(*cut)
    return factor_of


def deal_out(own_key, own, number, rows, count, top, bound, slope):
    ranking = jax.random.permutation(own_key, count)
    packed, common = portions_of(count, rows * top, bound, slope, True), portions_of(count, rows * top, bound, slope, False)
    places = jnp.arange(count)

    def named(sizes, turn):
        used = int((sizes > 0).sum())
        fixed = max(1, used // 4)
        shifted = fixed + (places - fixed + turn * (used - fixed)) % max(1, count - fixed)
        return jnp.zeros((count,), jnp.int32).at[ranking[jnp.where(places < fixed, places, shifted)]].set(jnp.asarray(sizes, jnp.int32))

    sizes = jnp.where(number % 4 == 0, named(packed, number // 4), named(common, number - number // 4 - 1))
    mixed = jax.random.permutation(jax.random.fold_in(own, 3), count)
    donor, receiver = mixed[0:count // 2 * 2:2], mixed[1:count // 2 * 2:2]
    room = jnp.minimum(sizes[donor] - 1, bound - sizes[receiver]) // 2
    room = jnp.where((donor == ranking[0]) | (receiver == ranking[0]) | (sizes[receiver] == 0), 0, jnp.maximum(room, 0))
    shifted = jax.random.randint(jax.random.fold_in(own, 4), (count // 2,), 0, 1 << 20) % (room + 1)
    sizes = sizes.at[donor].add(-shifted).at[receiver].add(shifted)
    labels = jnp.searchsorted(jnp.cumsum(sizes), jnp.arange(rows * top), side="right").astype(jnp.int32)
    grid = labels.reshape(top, rows).T
    grid = grid[jax.random.permutation(jax.random.fold_in(own, 1), rows)]
    turn = jax.random.randint(jax.random.fold_in(own, 2), (rows, 1), 0, top)
    return jnp.take_along_axis(grid, (jnp.arange(top)[None, :] + turn) % top, axis=1)


def portions_of(count, total, reach, slope, full):
    portions = [(1 << 20) // math.isqrt(rank ** slope) + 1 for rank in range(1, count + 1)]
    largest = reach if full else min(reach, max(-(-total // count), total * portions[0] // sum(portions)))
    least = 1 if total - largest >= count - 1 else 0
    counts, surplus = [largest] + [least] * (count - 1), total - largest - least * (count - 1)
    while surplus > 0:
        movable = [i for i in range(1, count) if counts[i] < largest] or [i for i in range(1, count) if counts[i] < reach]
        whole, left = sum([portions[i] for i in movable]), surplus
        for i in movable:
            addition = min(reach - counts[i], max(1, left * portions[i] // whole), surplus)
            counts[i] = counts[i] + addition
            surplus = surplus - addition
    return np.array(counts)


def bell_draw(key, extent, scale, limit, cuts=(), kind=jnp.bfloat16):
    values = jax.random.normal(key, extent, jnp.float32) * scale
    if len(cuts) > 0:
        values = level_of(key, extent, cuts, -0.22, 0.18) * values
    return jnp.clip(values, min=-limit, max=limit).astype(kind)


def setup_inputs(seed: int = 0) -> dict:
    splits = jax.random.split(jax.random.key(seed), 16)
    tokens = bell_draw(splits[0], (MICRO, SEQS, SLOT, D), 1.0, 6.0, ((1, 32),))
    lengths = draw_lengths(jax.random.fold_in(splits[15], 71), 0)
    routes_keys = jax.random.split(jax.random.fold_in(splits[2], 1), LAYERS * MICRO * SEQS * SLOT // SLOT)
    routes_turns = jax.random.permutation(jax.random.fold_in(splits[2], 3), LAYERS * MICRO * SEQS * SLOT // SLOT)
    routes = jax.vmap(lambda own, number: deal_out(jax.random.fold_in(splits[2], 2), own, number, SLOT, EXPERTS, 2, CAP, 1))(routes_keys, routes_turns).reshape((LAYERS, MICRO, SEQS, SLOT, 2))
    cotangent = bell_draw(splits[3], (MICRO, SEQS, SLOT, D), 1.0, 6.0, ((1, 32),))
    attn_gain = jnp.clip(1.0 + 0.1 * jax.random.normal(splits[4], (LAYERS, D), jnp.float32), 0.5, 1.5).astype(jnp.bfloat16)
    qkv_weight = bell_draw(splits[5], (LAYERS, D, 3 * D), D ** -0.5, 0.21875, ((1, 32),))
    out_weight = bell_draw(splits[6], (LAYERS, D, D), (D // 16) ** -0.5, 0.875, ((1, 32),))
    ffn_gain = jnp.clip(1.0 + 0.1 * jax.random.normal(splits[7], (LAYERS, D), jnp.float32), 0.5, 1.5).astype(jnp.bfloat16)
    router_weight = bell_draw(splits[8], (LAYERS, D, EXPERTS), (2 * D) ** -0.5, 0.15625, ((1, 32),))
    shared_gate = bell_draw(splits[9], (LAYERS, D, FF), D ** -0.5, 0.21875, ((1, 32),))
    shared_up = bell_draw(splits[10], (LAYERS, D, FF), D ** -0.5, 0.21875, ((1, 32),))
    shared_down = bell_draw(splits[11], (LAYERS, FF, D), FF ** -0.5, 0.125, ((1, 32),))
    expert_gate = bell_draw(splits[12], (LAYERS, EXPERTS, D, FF), D ** -0.5, 0.21875, ((1, 8), (3, 4)))
    expert_up = bell_draw(splits[13], (LAYERS, EXPERTS, D, FF), D ** -0.5, 0.21875, ((1, 8), (3, 4)))
    expert_down = bell_draw(splits[14], (LAYERS, EXPERTS, FF, D), FF ** -0.5, 0.125, ((1, 8), (2, 4)))
    return dict(tokens=tokens, lengths=lengths, routes=routes, cotangent=cotangent, attn_gain=attn_gain, qkv_weight=qkv_weight, out_weight=out_weight, ffn_gain=ffn_gain, router_weight=router_weight, shared_gate=shared_gate, shared_up=shared_up, shared_down=shared_down, expert_gate=expert_gate, expert_up=expert_up, expert_down=expert_down)


EPSILON = 1e-06
SCALE = 0.125
HIGHEST = lax.Precision.HIGHEST

@jax.custom_vjp
def low(v):
    return lax.optimization_barrier(v.astype(jnp.bfloat16)).astype(jnp.float32)

@jax.custom_vjp
def low_back(v):
    return v

def low_keep(v):
    return (low(v), None)

def low_pass(kept, grad):
    return (grad,)

def back_keep(v):
    return (v, None)

def back_low(kept, grad):
    return (low(grad),)
low.defvjp(low_keep, low_pass)
low_back.defvjp(back_keep, back_low)

def matmul(left_side, right_side):
    return jnp.dot(left_side, right_side, precision=HIGHEST)

def rms_norm(hidden, gain_vector):
    return hidden * lax.rsqrt(lax.optimization_barrier(jnp.mean(hidden * hidden, axis=-1, keepdims=True)) + EPSILON) * gain_vector

def rope_tables(row_count, head_width):
    middle = head_width // 2
    frequency = jnp.exp(jnp.arange(middle, dtype=jnp.float32) * (-2.0 * math.log(10000.0) / head_width))
    angles = jnp.arange(row_count, dtype=jnp.float32)[:, None] * frequency[None, :]
    return (jnp.cos(angles), jnp.sin(angles))

def rotate(head_values, cosine, sine_table):
    middle = head_values.shape[-1] // 2
    first_half = head_values[..., :middle]
    second_half = head_values[..., middle:]
    cos_table = cosine[:, None, :]
    sin_table = sine_table[:, None, :]
    return jnp.concatenate([first_half * cos_table - second_half * sin_table, second_half * cos_table + first_half * sin_table], axis=-1)

def allowed_mask(row_count, length):
    places = jnp.arange(row_count)
    return (places[None, :] <= places[:, None]) & (places[None, :] < length)

def gate_values(logits, choices):
    highest = lax.optimization_barrier(jnp.max(logits, axis=-1, keepdims=True))
    exponent = jnp.exp(logits - highest)
    probability = exponent / lax.optimization_barrier(jnp.sum(exponent, axis=-1, keepdims=True))
    picked = jnp.take_along_axis(probability, choices, axis=-1)
    return picked / lax.optimization_barrier(jnp.sum(picked, axis=-1, keepdims=True))

def positions(choices, expert_count):
    flat_ids = choices.reshape(-1)
    matches = (flat_ids[:, None] == jnp.arange(expert_count)[None, :]).astype(jnp.int32)
    before = jnp.cumsum(matches, axis=0) - matches
    return lax.optimization_barrier(jnp.sum(before * matches, axis=1)).reshape(choices.shape).astype(jnp.int32)

def attend(normed, qkv_weight, length, cosine, sine_table):
    row_count = normed.shape[0]
    projected = low_back(matmul(normed, qkv_weight)).reshape(row_count, 3, HEADS, HDIM)
    queries = low(rotate(projected[:, 0], cosine, sine_table))
    key_rows = low(rotate(projected[:, 1], cosine, sine_table))
    values = low(projected[:, 2])
    scores = low_back(jnp.einsum('qhd,khd->hqk', queries, key_rows, precision=HIGHEST) * SCALE)
    scores = jnp.where(allowed_mask(row_count, length)[None], scores, -1e+30)
    highest = lax.optimization_barrier(jnp.max(scores, axis=-1, keepdims=True))
    exponent = jnp.exp(scores - highest)
    probability = exponent / lax.optimization_barrier(jnp.sum(exponent, axis=-1, keepdims=True))
    mixture = jnp.einsum('hqk,khd->qhd', low(probability), values, precision=HIGHEST)
    return low(low_back(mixture)).reshape(row_count, HEADS * HDIM)

def swiglu_hidden(row_block, gate_weight, up_weight):
    gate_part = low_back(matmul(row_block, gate_weight))
    up_part = low_back(matmul(row_block, up_weight))
    return low(jax.nn.silu(gate_part) * up_part)

def expert_apply(pieces):
    row_block, gate_weight, up_weight, down_weight = pieces
    return low(low_back(matmul(swiglu_hidden(row_block, gate_weight, up_weight), down_weight)))

def fill_buffer(first_rows, second_rows, choices, slot_index):
    buffer = jnp.zeros((EXPERTS, CAP, first_rows.shape[-1]), first_rows.dtype)
    buffer = buffer.at[choices[:, 0], slot_index[:, 0]].set(first_rows)
    return buffer.at[choices[:, 1], slot_index[:, 1]].set(second_rows)

def pick_rows(produced, choices, slot_index):
    return produced[choices, slot_index]

def layer_forward(hidden, slot_lengths, choices, slot_index, params):
    attn_gain, qkv_weight, out_weight, ffn_gain, router_weight, shared_gate, shared_up, shared_down, expert_gate, expert_up, expert_down = params
    slot_count = hidden.shape[0]
    group_size = math.gcd(slot_count, max(1, 4096 // SLOT))
    cosine, sine_table = rope_tables(SLOT, HDIM)
    normed_attn = low(rms_norm(hidden, attn_gain))

    def group_attend(pieces):
        blocks, block_lengths = pieces
        return jax.vmap(attend, in_axes=(0, None, 0, None, None))(blocks, qkv_weight, block_lengths, cosine, sine_table)
    mixture = lax.map(jax.checkpoint(group_attend), (normed_attn.reshape(-1, group_size, SLOT, D), slot_lengths.reshape(-1, group_size)))
    mixture = mixture.reshape(slot_count, SLOT, D)
    after_attn = hidden + low_back(matmul(mixture, out_weight))
    normed_ffn = low(rms_norm(after_attn, ffn_gain))
    gate_share = gate_values(low_back(matmul(normed_ffn, router_weight)), choices)
    first_rows = low_back(normed_ffn)
    second_rows = low_back(normed_ffn)
    buffer = jax.vmap(fill_buffer)(first_rows, second_rows, choices, slot_index)
    by_expert = jnp.swapaxes(buffer, 0, 1).reshape(EXPERTS, slot_count * CAP, D)
    produced = lax.map(jax.checkpoint(expert_apply), (by_expert, expert_gate, expert_up, expert_down))
    produced = jnp.swapaxes(produced.reshape(EXPERTS, slot_count, CAP, D), 0, 1)
    picked = jax.vmap(pick_rows)(produced, choices, slot_index)
    routed = gate_share[..., 0:1] * picked[:, :, 0] + gate_share[..., 1:2] * picked[:, :, 1]
    shared_out = low_back(matmul(swiglu_hidden(normed_ffn, shared_gate, shared_up), shared_down))
    return after_attn + routed + shared_out

def reference(tokens, lengths, routes, cotangent, attn_gain, qkv_weight, out_weight, ffn_gain, router_weight, shared_gate, shared_up, shared_down, expert_gate, expert_up, expert_down):
    slot_count = MICRO * SEQS
    hidden = tokens.astype(jnp.float32).reshape(slot_count, SLOT, D)
    slot_lengths = lengths.reshape(slot_count)
    choices = routes.reshape(LAYERS, slot_count, SLOT, 2)
    slot_index = jax.vmap(jax.vmap(partial(positions, expert_count=EXPERTS)))(choices)
    params = tuple((weight.astype(jnp.float32) for weight in (attn_gain, qkv_weight, out_weight, ffn_gain, router_weight, shared_gate, shared_up, shared_down, expert_gate, expert_up, expert_down)))

    def forward(start_state, weights):
        current = start_state
        for layer_index in range(LAYERS):
            layer_params = tuple((weight[layer_index] for weight in weights))
            current = layer_forward(current, slot_lengths, choices[layer_index], slot_index[layer_index], layer_params)
        return current
    result, pullback = jax.vjp(forward, hidden, params)
    valid_rows = (jnp.arange(SLOT)[None, :] < slot_lengths[:, None]).astype(jnp.float32)
    seed_grad = cotangent.astype(jnp.float32).reshape(slot_count, SLOT, D) * valid_rows[..., None]
    grad_start, gradients = pullback(seed_grad)
    out_shape = (MICRO, SEQS, SLOT, D)
    return (result.reshape(out_shape), grad_start.reshape(out_shape), gradients[0], gradients[1], gradients[2], gradients[3], gradients[4], gradients[5], gradients[6], gradients[7], gradients[8], gradients[9], gradients[10])
```

```python
from functools import partial
import math

import jax
import jax.numpy as jnp
from jax import lax
from jax.sharding import Mesh, PartitionSpec as P

HEADS = 12
HDIM = 64
LAYERS = 2
MICRO = 2
SLOT = 128
EPSILON = 1e-06
SCALE = 0.125

DP = ("y", "x", "core")
LINE = "z"
ALL = ("y", "x", "core", "z")


def contract_first(left_side, right_side):
    return lax.dot_general(
        left_side, right_side, (((0,), (0,)), ((), ())), preferred_element_type=jnp.float32
    )


def contract_last(left_side, right_side):
    return lax.dot_general(
        left_side, right_side, (((1,), (1,)), ((), ())), preferred_element_type=jnp.float32
    )


def matmul(left_side, right_side):
    return jnp.dot(left_side, right_side, preferred_element_type=jnp.float32)


def low(value):
    return value.astype(jnp.bfloat16)


def shift(value, axis, step):
    size = lax.axis_size(axis)
    return lax.ppermute(value, axis, [(i, (i + step) % size) for i in range(size)])


def gather_axis(value, axis, place):
    size = lax.axis_size(axis)
    me = lax.axis_index(axis)
    pieces = [value] + [shift(value, axis, step) for step in range(1, size)]
    ordered = []
    for index in range(size):
        source = (me - index) % size
        chosen = pieces[0]
        for step in range(1, size):
            chosen = jnp.where(source == step, pieces[step], chosen)
        ordered.append(chosen)
    return jnp.stack(ordered, axis=place)


def scatter_axis(value, axis, place, out_type):
    size = lax.axis_size(axis)
    me = lax.axis_index(axis)
    total = lax.dynamic_index_in_dim(value, me, place, keepdims=False).astype(jnp.float32)
    for step in range(1, size):
        block = lax.dynamic_index_in_dim(value, (me + step) % size, place, keepdims=False)
        total = total + shift(block, axis, step).astype(jnp.float32)
    return total.astype(out_type)


def gather_plane(value, first_x):
    if first_x:
        value = gather_axis(value, "x", 0)
        value = gather_axis(value, "y", 0)
    else:
        value = gather_axis(value, "y", 0)
        value = gather_axis(value, "x", 1)
    return gather_axis(value, "core", 2)


def scatter_plane(value, first_x, out_type):
    value = scatter_axis(value, "core", 2, jnp.bfloat16)
    if first_x:
        value = scatter_axis(value, "x", 1, jnp.bfloat16)
        return scatter_axis(value, "y", 0, out_type)
    value = scatter_axis(value, "y", 0, jnp.bfloat16)
    return scatter_axis(value, "x", 0, out_type)


def gather_rows(shard, first_x):
    cols = shard.shape[-1]
    return gather_plane(gather_axis(shard, LINE, 0), first_x).reshape(-1, cols)


def scatter_rows(value, first_x):
    sizes = [lax.axis_size(axis) for axis in ALL]
    value = value.reshape(*sizes, -1, value.shape[-1])
    value = scatter_plane(value, first_x, jnp.bfloat16)
    return scatter_axis(value, LINE, 0, jnp.float32)


def line_blocks(value):
    return [value] + [shift(value, LINE, step) for step in range(1, lax.axis_size(LINE))]


def line_sum(blocks):
    total = blocks[0]
    for step in range(1, lax.axis_size(LINE)):
        total = total + shift(low(blocks[step]), LINE, -step).astype(jnp.float32)
    return total


def swap_experts(value):
    return lax.all_to_all(value, DP, split_axis=0, concat_axis=0, tiled=True)


def rms_scale(hidden):
    return lax.rsqrt(jnp.mean(hidden * hidden, axis=-1, keepdims=True) + EPSILON)


def rms_norm(hidden, gain_vector):
    return hidden * rms_scale(hidden) * gain_vector


def rms_back(hidden, gain_vector, grad):
    scale = rms_scale(hidden)
    unit = hidden * scale
    grad_gain = jnp.sum(grad * unit, axis=0)
    grad_unit = grad * gain_vector
    inner = jnp.mean(grad_unit * unit, axis=-1, keepdims=True)
    return (scale * (grad_unit - unit * inner), grad_gain)


def rope_tables(row_count, head_width):
    middle = head_width // 2
    frequency = jnp.exp(
        jnp.arange(middle, dtype=jnp.float32) * (-2.0 * math.log(10000.0) / head_width)
    )
    angles = jnp.arange(row_count, dtype=jnp.float32)[:, None] * frequency[None, :]
    return (jnp.cos(angles), jnp.sin(angles))


def rotate(head_values, cosine, sine_table):
    middle = head_values.shape[-1] // 2
    first_half = head_values[..., :middle]
    second_half = head_values[..., middle:]
    cos_table = cosine[:, None, :]
    sin_table = sine_table[:, None, :]
    return jnp.concatenate(
        [
            first_half * cos_table - second_half * sin_table,
            second_half * cos_table + first_half * sin_table,
        ],
        axis=-1,
    )


def masked_scores(queries, key_rows, length):
    scores = (
        jnp.einsum("qhd,khd->hqk", queries, key_rows, preferred_element_type=jnp.float32) * SCALE
    )
    places = jnp.arange(queries.shape[0])
    allowed = (places[None, :] <= places[:, None]) & (places[None, :] < length)
    return jnp.where(allowed[None], scores, -1e30)


def attention_front(normed, qkv_full, length, tables):
    row_count = normed.shape[0]
    projected = matmul(normed, qkv_full).reshape(row_count, 3, HEADS, HDIM)
    queries = low(rotate(projected[:, 0], *tables))
    key_rows = low(rotate(projected[:, 1], *tables))
    values = low(projected[:, 2])
    scores = masked_scores(queries, key_rows, length)
    highest = jnp.max(scores, axis=-1, keepdims=True)
    exponent = jnp.exp(scores - highest)
    totals = jnp.sum(exponent, axis=-1, keepdims=True)
    mixture = jnp.einsum(
        "hqk,khd->qhd", low(exponent / totals), values, preferred_element_type=jnp.float32
    )
    return (
        low(mixture).reshape(row_count, HEADS * HDIM),
        queries,
        key_rows,
        values,
        highest + jnp.log(totals),
    )


def attention_back(grad_mixture, qkv_full, queries, key_rows, values, log_total, length, tables):
    row_count = queries.shape[0]
    grad_heads = low(grad_mixture.reshape(row_count, HEADS, HDIM))
    probability = jnp.exp(masked_scores(queries, key_rows, length) - log_total)
    grad_prob = jnp.einsum("qhd,khd->hqk", grad_heads, values, preferred_element_type=jnp.float32)
    grad_values = jnp.einsum(
        "hqk,qhd->khd", low(probability), grad_heads, preferred_element_type=jnp.float32
    )
    inner = jnp.sum(probability * grad_prob, axis=-1, keepdims=True)
    grad_scores = low(probability * (grad_prob - inner))
    grad_queries = (
        jnp.einsum("hqk,khd->qhd", grad_scores, key_rows, preferred_element_type=jnp.float32)
        * SCALE
    )
    grad_keys = (
        jnp.einsum("hqk,qhd->khd", grad_scores, queries, preferred_element_type=jnp.float32) * SCALE
    )
    cosine, sine_table = tables
    grad_projected = jnp.stack(
        [
            rotate(grad_queries, cosine, -sine_table),
            rotate(grad_keys, cosine, -sine_table),
            grad_values,
        ],
        axis=1,
    )
    grad_projected = low(grad_projected.reshape(row_count, 3 * HEADS * HDIM))
    return (contract_last(grad_projected, qkv_full), grad_projected)


def swiglu_front(rows, gate_up):
    both = matmul(rows, gate_up)
    gate_part, up_part = jnp.split(both, 2, axis=1)
    return (gate_part, up_part, low(jax.nn.silu(gate_part) * up_part))


def swiglu_back(grad_low, down, gate_part, up_part):
    grad_hidden = contract_last(grad_low, down)
    sigma = jax.nn.sigmoid(gate_part)
    grad_gate = low(grad_hidden * up_part * sigma * (1.0 + gate_part * (1.0 - sigma)))
    grad_up = low(grad_hidden * (gate_part * sigma))
    return jnp.concatenate([grad_gate, grad_up], axis=1)


def destinations(routes, expert_count, capacity, line_size):
    layers, micro, rows, top = routes.shape
    flat = routes.reshape(layers, micro, rows * top)
    matches = low(flat[..., None] == jnp.arange(expert_count))
    places = jnp.arange(rows * top)
    earlier = low(places[None, :] < places[:, None])
    before = jnp.einsum("pq,lmqe->lmpe", earlier, matches, preferred_element_type=jnp.float32)
    index = jnp.sum(before * matches.astype(jnp.float32), axis=-1).astype(jnp.int32)
    place = flat * (capacity * line_size) + index
    return jnp.swapaxes(place.reshape(layers, micro, rows, top), 2, 3)


def on_device(
    tokens,
    lengths,
    routes,
    cotangent,
    attn_gain,
    qkv_weight,
    out_weight,
    ffn_gain,
    router_weight,
    shared_gate,
    shared_up,
    shared_down,
    expert_gate,
    expert_up,
    expert_down,
):
    line_size = lax.axis_size(LINE)
    line_place = lax.axis_index(LINE)
    dp_size = lax.axis_size(DP)
    expert_count = dp_size
    capacity = 9 * SLOT // (4 * expert_count)
    block_rows = capacity * line_size
    width = tokens.shape[-1]
    rows_owned = qkv_weight.shape[1]
    hidden_owned = shared_down.shape[1]
    hidden_slice = dp_size * hidden_owned
    tables = rope_tables(SLOT, HDIM)

    small = []
    for layer in range(LAYERS):
        small += [router_weight[layer], attn_gain[layer][:, None], ffn_gain[layer][:, None]]
    small = jnp.concatenate(small, axis=1)
    small_cols = small.shape[1]
    small = jnp.pad(small, ((0, 0), (0, 128 - small_cols)))
    small_full = gather_rows(small, True).T
    per_layer = expert_count + 2

    def gather_attention(layer):
        qkv = qkv_weight[layer]
        half = qkv.shape[1] // 2
        qkv_full = jnp.concatenate(
            [gather_rows(qkv[:, :half], True), gather_rows(qkv[:, half:], False)], axis=1
        )
        return (qkv_full, gather_rows(out_weight[layer], False))

    def gather_shared(layer):
        parts = []
        for weight in (shared_gate[layer], shared_up[layer]):
            parts.append(weight.reshape(rows_owned, dp_size, line_size, hidden_owned))
        both = jnp.stack(parts, axis=1)
        pieces = []
        for step in range(line_size):
            piece = lax.dynamic_index_in_dim(
                both, (line_place + step) % line_size, 3, keepdims=False
            ).reshape(rows_owned, 2 * hidden_slice)
            pieces.append(piece if step == 0 else shift(piece, LINE, step))
        ordered = []
        for index in range(line_size):
            source = (line_place - index) % line_size
            chosen = pieces[0]
            for step in range(1, line_size):
                chosen = jnp.where(source == step, pieces[step], chosen)
            ordered.append(chosen)
        gate_up = gather_plane(jnp.stack(ordered), False).reshape(width, 2 * hidden_slice)
        down = gather_plane(shared_down[layer], True).reshape(hidden_slice, width)
        return (gate_up, down)

    attention_weights = [None] * LAYERS
    shared_weights = [None] * LAYERS
    for layer in range(LAYERS):
        attention_weights[layer] = gather_attention(layer)
        shared_weights[layer] = gather_shared(layer)
    small_weights = []
    for layer in range(LAYERS):
        mine = small_full[layer * per_layer : (layer + 1) * per_layer]
        small_weights.append(
            (
                mine[:expert_count],
                mine[expert_count].astype(jnp.float32),
                mine[expert_count + 1].astype(jnp.float32),
            )
        )
    expert_weights = [
        (
            jnp.concatenate([expert_gate[layer, 0], expert_up[layer, 0]], axis=1),
            expert_down[layer, 0],
        )
        for layer in range(LAYERS)
    ]

    own_routes = routes[:, :, 0]
    place = destinations(own_routes, expert_count, capacity, line_size)
    routing = jnp.stack([place, jnp.swapaxes(own_routes, 2, 3)])
    routing = line_blocks(routing)
    place_line = jnp.concatenate(
        [block[0] + step * capacity for step, block in enumerate(routing)], axis=-1
    )
    choice_line = jnp.concatenate([block[1] for block in routing], axis=-1)
    buffer_rows = expert_count * block_rows

    def pick_masks(layer, micro):
        target = place_line[layer, micro]
        rows = jnp.arange(buffer_rows)[:, None]
        return (rows == target[0][None, :], rows == target[1][None, :])

    def gates_of(logits, choices):
        highest = jnp.max(logits, axis=0, keepdims=True)
        exponent = jnp.exp(logits - highest)
        probability = exponent / jnp.sum(exponent, axis=0, keepdims=True)
        experts = jnp.arange(expert_count)[:, None]
        picked = jnp.stack(
            [
                jnp.sum(jnp.where(experts == choices[k][None, :], probability, 0.0), axis=0)
                for k in range(2)
            ]
        )
        return picked / jnp.sum(picked, axis=0, keepdims=True)

    def forward_micro(layer, micro, current):
        qkv_full, out_full = attention_weights[layer]
        shared_gate_up, shared_down_full = shared_weights[layer]
        router_t, gain_attn, gain_ffn = small_weights[layer]
        gate_up, down = expert_weights[layer]
        length = lengths[micro, 0]
        normed_attn = low(rms_norm(current, gain_attn))
        mixture, queries, key_rows, values, log_total = attention_front(
            normed_attn, qkv_full, length, tables
        )
        after_attn = current + matmul(mixture, out_full)
        normed_ffn = low(rms_norm(after_attn, gain_ffn))
        line_rows = jnp.concatenate(line_blocks(normed_ffn), axis=0)
        first, second = pick_masks(layer, micro)
        outbound = low(matmul(low(first | second), line_rows))
        arrived = swap_experts(outbound.reshape(expert_count, block_rows, width))
        arrived = arrived.reshape(buffer_rows, width)
        logits = contract_last(router_t, line_rows)
        gates, gate_pull = jax.vjp(
            partial(gates_of, choices=choice_line[layer, micro]), logits
        )
        mixing = low(
            jnp.where(first, gates[0][None, :], 0.0) + jnp.where(second, gates[1][None, :], 0.0)
        )
        shared_record = swiglu_front(line_rows, shared_gate_up)
        shared_out = matmul(shared_record[2], shared_down_full)
        expert_record = swiglu_front(arrived, gate_up)
        produced = low(matmul(expert_record[2], down))
        returned = swap_experts(produced.reshape(expert_count, block_rows, width))
        returned = returned.reshape(buffer_rows, width)
        partial_out = contract_first(mixing, returned) + shared_out
        result = after_attn + line_sum(jnp.split(partial_out, line_size, axis=0))
        record = (
            current,
            after_attn,
            normed_attn,
            mixture,
            queries,
            key_rows,
            values,
            log_total,
            line_rows,
            gate_pull,
            mixing,
            returned,
            shared_record,
            arrived,
            expert_record,
        )
        return (record, result)

    def backward_micro(layer, micro, grad_out, record):
        (
            current,
            after_attn,
            normed_attn,
            mixture,
            queries,
            key_rows,
            values,
            log_total,
            line_rows,
            gate_pull,
            mixing,
            returned,
            shared_record,
            arrived,
            expert_record,
        ) = record
        qkv_full, out_full = attention_weights[layer]
        shared_gate_up, shared_down_full = shared_weights[layer]
        router_t, gain_attn, gain_ffn = small_weights[layer]
        gate_up, down = expert_weights[layer]
        grad_line = jnp.concatenate(line_blocks(low(grad_out)), axis=0)
        outbound = low(matmul(mixing, grad_line))
        grad_in = swap_experts(outbound.reshape(expert_count, block_rows, width))
        grad_in = grad_in.reshape(buffer_rows, width)
        shared_grads = swiglu_back(grad_line, shared_down_full, shared_record[0], shared_record[1])
        shared_rows = contract_last(shared_grads, shared_gate_up)
        first, second = pick_masks(layer, micro)
        products = contract_last(returned, grad_line)
        grad_gates = jnp.stack(
            [
                jnp.sum(jnp.where(first, products, 0.0), axis=0),
                jnp.sum(jnp.where(second, products, 0.0), axis=0),
            ]
        )
        grad_logits = low(gate_pull(grad_gates)[0])
        shared_rows = shared_rows + contract_first(grad_logits, router_t)
        grad_router = matmul(grad_logits, line_rows)
        expert_grads = swiglu_back(grad_in, down, expert_record[0], expert_record[1])
        grad_rows = low(contract_last(expert_grads, gate_up))
        back = swap_experts(grad_rows.reshape(expert_count, block_rows, width))
        back = back.reshape(buffer_rows, width)
        partial_grad = contract_first(low(first | second), back) + shared_rows
        grad_ffn = line_sum(jnp.split(partial_grad, line_size, axis=0))
        grad_after_norm, grad_gain_ffn = rms_back(after_attn, gain_ffn, grad_ffn)
        grad_after = grad_out + grad_after_norm
        grad_attn = low(grad_after)
        grad_mixture = contract_last(grad_attn, out_full)
        grad_normed, grad_projected = attention_back(
            grad_mixture, qkv_full, queries, key_rows, values, log_total, length=lengths[micro, 0],
            tables=tables,
        )
        grad_current, grad_gain_attn = rms_back(current, gain_attn, grad_normed)
        pairs = (
            (normed_attn, grad_projected),
            (mixture, grad_attn),
            (line_rows, shared_grads),
            (shared_record[2], grad_line),
            (arrived, expert_grads),
            (expert_record[2], grad_in),
        )
        return (grad_after + grad_current, (grad_router, grad_gain_attn, grad_gain_ffn), pairs)

    states = [tokens[micro, 0].astype(jnp.float32) for micro in range(MICRO)]
    records = []
    for layer in range(LAYERS):
        layer_records = []
        for micro in range(MICRO):
            record, states[micro] = forward_micro(layer, micro, states[micro])
            layer_records.append(record)
        records.append(layer_records)
    output = jnp.stack(states)[:, None]

    places = jnp.arange(SLOT)
    flowing = [
        cotangent[micro, 0].astype(jnp.float32)
        * (places < lengths[micro, 0]).astype(jnp.float32)[:, None]
        for micro in range(MICRO)
    ]
    owned = [None] * LAYERS
    small_grads = [None] * LAYERS
    for layer in reversed(range(LAYERS)):
        small_total = None
        all_pairs = []
        for micro in range(MICRO):
            flowing[micro], small_terms, pairs = backward_micro(
                layer, micro, flowing[micro], records[layer][micro]
            )
            all_pairs.append(pairs)
            small_total = (
                small_terms
                if small_total is None
                else jax.tree.map(jnp.add, small_total, small_terms)
            )
        terms = [
            contract_first(
                jnp.concatenate([pairs[member][0] for pairs in all_pairs], axis=0),
                jnp.concatenate([pairs[member][1] for pairs in all_pairs], axis=0),
            )
            for member in range(6)
        ]
        grad_qkv, grad_out, grad_gate_up, grad_down = [low(term) for term in terms[:4]]
        half = grad_qkv.shape[1] // 2
        qkv_owned = jnp.concatenate(
            [scatter_rows(grad_qkv[:, :half], True), scatter_rows(grad_qkv[:, half:], False)],
            axis=1,
        )
        out_owned = scatter_rows(grad_out, False)
        sizes = [lax.axis_size(axis) for axis in ALL]
        gate_up_rows = scatter_plane(
            grad_gate_up.reshape(*sizes, rows_owned, 2 * hidden_slice), False, jnp.bfloat16
        )
        down_owned = scatter_plane(
            grad_down.reshape(*sizes[:3], hidden_owned, width), True, jnp.float32
        )
        pieces = []
        for step in range(line_size):
            piece = lax.dynamic_index_in_dim(
                gate_up_rows, (line_place + step) % line_size, 0, keepdims=False
            )
            pieces.append(piece if step == 0 else shift(piece, LINE, step))
        ordered = []
        for index in range(line_size):
            source = (line_place - index) % line_size
            chosen = pieces[0]
            for step in range(1, line_size):
                chosen = jnp.where(source == step, pieces[step], chosen)
            ordered.append(chosen.reshape(rows_owned, 2, dp_size, hidden_owned))
        gate_up_owned = jnp.stack(ordered, axis=3).reshape(rows_owned, 2, -1).astype(jnp.float32)
        inner = hidden_slice
        owned[layer] = (
            qkv_owned,
            out_owned,
            gate_up_owned[:, 0],
            gate_up_owned[:, 1],
            down_owned,
            terms[4][:, : terms[4].shape[1] // 2],
            terms[4][:, terms[4].shape[1] // 2 :],
            terms[5],
        )
        small_grads[layer] = small_total
    small_rows = []
    for layer in range(LAYERS):
        grad_router, grad_gain_attn, grad_gain_ffn = small_grads[layer]
        small_rows += [grad_router, grad_gain_attn[None], grad_gain_ffn[None]]
    small_rows = jnp.concatenate(small_rows, axis=0)
    small_rows = jnp.pad(small_rows, ((0, 128 - small_rows.shape[0]), (0, 0)))
    small_owned = scatter_rows(low(small_rows.T), True)
    router_owned = []
    gain_attn_owned = []
    gain_ffn_owned = []
    for layer in range(LAYERS):
        mine = small_owned[:, layer * per_layer : (layer + 1) * per_layer]
        router_owned.append(mine[:, :expert_count])
        gain_attn_owned.append(mine[:, expert_count])
        gain_ffn_owned.append(mine[:, expert_count + 1])
    input_grad = jnp.stack(flowing)[:, None]
    stacked = [
        jnp.stack([owned[layer][member] for layer in range(LAYERS)]) for member in range(8)
    ]
    return (
        output,
        input_grad,
        jnp.stack(gain_attn_owned),
        stacked[0],
        stacked[1],
        jnp.stack(gain_ffn_owned),
        jnp.stack(router_owned),
        stacked[2],
        stacked[3],
        stacked[4],
        stacked[5][:, None],
        stacked[6][:, None],
        stacked[7][:, None],
    )


def solution(mesh):
    dp_size, line_size = mesh.devices.shape
    fine = Mesh(mesh.devices.reshape(dp_size // 4, 2, 2, line_size), ALL)
    rows_of = {
        2: P(None, ALL),
        3: P(None, ALL, None),
        4: P(None, ALL, None, None),
    }
    in_specs = (
        rows_of[4],
        rows_of[2],
        P(None, None, ALL, None, None),
        rows_of[4],
        rows_of[2],
        rows_of[3],
        rows_of[3],
        rows_of[2],
        rows_of[3],
        rows_of[3],
        rows_of[3],
        rows_of[3],
        P(None, DP, None, LINE),
        P(None, DP, None, LINE),
        P(None, DP, LINE, None),
    )
    out_specs = (
        rows_of[4],
        rows_of[4],
        rows_of[2],
        rows_of[3],
        rows_of[3],
        rows_of[2],
        rows_of[3],
        rows_of[3],
        rows_of[3],
        rows_of[3],
        P(None, DP, None, LINE),
        P(None, DP, None, LINE),
        P(None, DP, LINE, None),
    )
    return jax.shard_map(
        on_device, mesh=fine, in_specs=in_specs, out_specs=out_specs, check_vma=False
    )
```

```python
import math

import jax
import jax.numpy as jnp
from jax import lax
from jax.experimental import pallas as pl
from jax.experimental.pallas import tpu as pltpu
from jax.sharding import Mesh, PartitionSpec as P

HEADS = 12
HDIM = 64
LAYERS = 2
MICRO = 2
SLOT = 128
EPSILON = 1e-06
SCALE = 0.125

DP = ("y", "x", "core")
LINE = "z"
ALL = ("y", "x", "core", "z")
PAIR = 2 * HDIM
F32 = jnp.float32
BF16 = jnp.bfloat16


def contract_first(left_side, right_side):
    return lax.dot_general(
        left_side, right_side, (((0,), (0,)), ((), ())), preferred_element_type=jnp.float32
    )


def contract_last(left_side, right_side):
    return lax.dot_general(
        left_side, right_side, (((1,), (1,)), ((), ())), preferred_element_type=jnp.float32
    )


def matmul(left_side, right_side):
    return jnp.dot(left_side, right_side, preferred_element_type=jnp.float32)


def low(value):
    return value.astype(jnp.bfloat16)


def shift(value, axis, step):
    size = lax.axis_size(axis)
    return lax.ppermute(value, axis, [(i, (i + step) % size) for i in range(size)])


def gather_axis(value, axis, place):
    size = lax.axis_size(axis)
    me = lax.axis_index(axis)
    pieces = [value] + [shift(value, axis, step) for step in range(1, size)]
    ordered = []
    for index in range(size):
        source = (me - index) % size
        chosen = pieces[0]
        for step in range(1, size):
            chosen = jnp.where(source == step, pieces[step], chosen)
        ordered.append(chosen)
    return jnp.stack(ordered, axis=place)


def scatter_axis(value, axis, place, out_type):
    size = lax.axis_size(axis)
    me = lax.axis_index(axis)
    total = lax.dynamic_index_in_dim(value, me, place, keepdims=False).astype(jnp.float32)
    for step in range(1, size):
        block = lax.dynamic_index_in_dim(value, (me + step) % size, place, keepdims=False)
        total = total + shift(block, axis, step).astype(jnp.float32)
    return total.astype(out_type)


def order_axis(mine, other, axis, place):
    me = lax.axis_index(axis)
    blocks = [mine] + other
    size = len(blocks)
    ordered = []
    for index in range(size):
        source = (me - index) % size
        chosen = blocks[0]
        for step in range(1, size):
            chosen = jnp.where(source == step, blocks[step], chosen)
        ordered.append(chosen)
    return jnp.stack(ordered, axis=place)


def send_axis(value, axis):
    return [shift(value, axis, step) for step in range(1, lax.axis_size(axis))]


def gather_line(pieces, place):
    size = lax.axis_size(LINE)
    me = lax.axis_index(LINE)
    ordered = []
    for index in range(size):
        source = (me - index) % size
        chosen = pieces[0]
        for step in range(1, size):
            chosen = jnp.where(source == step, pieces[step], chosen)
        ordered.append(chosen)
    return jnp.stack(ordered, axis=place)


def exchange_line(blocks, place):
    size = lax.axis_size(LINE)
    me = lax.axis_index(LINE)
    pieces = []
    for step in range(size):
        piece = lax.dynamic_index_in_dim(blocks, (me + step) % size, 0, keepdims=False)
        pieces.append(piece if step == 0 else shift(piece, LINE, step))
    return gather_line(pieces, place)


def after(value, *earlier):
    return lax.optimization_barrier((value, earlier))[0]


def line_blocks(value):
    return [value] + [shift(value, LINE, step) for step in range(1, lax.axis_size(LINE))]


def line_return(blocks):
    return [blocks[0]] + [shift(blocks[step], LINE, -step) for step in range(1, len(blocks))]


def swap_experts(value, expert_count):
    rows, cols = value.shape
    value = value.reshape(expert_count, rows // expert_count, cols)
    value = lax.all_to_all(value, DP, split_axis=0, concat_axis=0, tiled=True)
    return value.reshape(rows, cols)


def one_block(shape, place):
    return pl.BlockSpec(
        shape, lambda step: place, memory_space=pltpu.VMEM, pipeline_mode=pl.Buffered(1)
    )


def layer_block(array, layer):
    shape = array.shape[1:]
    while len(shape) > 2:
        shape = shape[1:]
    lead = (None,) * (array.ndim - 2)
    place = (layer,) + (0,) * (array.ndim - 1)
    return (array, one_block(lead + shape, place))


def scalars(array):
    return (array, pl.BlockSpec(memory_space=pltpu.SMEM))


def run(body, outs, operands, order=(), flops=0):
    blocked = any(isinstance(op, tuple) and op[1].block_shape is not None for op in operands)
    operands = [
        op if isinstance(op, tuple) else (op, pl.BlockSpec(memory_space=pltpu.VMEM))
        for op in operands
    ]
    order = [jax.tree.leaves(item)[0] for item in order]
    count = len(operands)

    def kernel(*refs):
        body(*refs[:count], *refs[count + len(order) :])

    size = sum(math.prod(op.shape) * op.dtype.itemsize for op, _ in operands)
    size += sum(math.prod(shape) * jnp.dtype(kind).itemsize for shape, kind in outs)
    return pl.pallas_call(
        kernel,
        out_shape=[jax.ShapeDtypeStruct(shape, kind) for shape, kind in outs],
        in_specs=[spec for _, spec in operands] + [pl.BlockSpec(memory_space=pl.ANY)] * len(order),
        out_specs=[pl.BlockSpec(memory_space=pltpu.VMEM)] * len(outs),
        grid=(1,) if blocked else (),
        compiler_params=pltpu.CompilerParams(vmem_limit_bytes=48 * 1024 * 1024),
        cost_estimate=pl.CostEstimate(flops=int(flops), bytes_accessed=int(size), transcendentals=0),
    )(*[op for op, _ in operands], *order)


def rms_scale(hidden):
    return lax.rsqrt(jnp.mean(hidden * hidden, axis=-1, keepdims=True) + EPSILON)


def rms_back(hidden, gain_vector, grad):
    scale = rms_scale(hidden)
    unit = hidden * scale
    grad_gain = jnp.sum(grad * unit, axis=0, keepdims=True)
    grad_unit = grad * gain_vector
    inner = jnp.mean(grad_unit * unit, axis=-1, keepdims=True)
    return (scale * (grad_unit - unit * inner), grad_gain)


def rope_tables(row_count):
    middle = HDIM // 2
    frequency = jnp.exp(jnp.arange(middle, dtype=F32) * (-2.0 * math.log(10000.0) / HDIM))
    angles = jnp.arange(row_count, dtype=F32)[:, None] * frequency[None, :]
    cosine, sine = (jnp.cos(angles), jnp.sin(angles))
    return (
        jnp.concatenate([cosine] * 4, axis=1),
        jnp.concatenate([-sine, sine, -sine, sine], axis=1),
    )


def half_turn(values):
    lane = lax.broadcasted_iota(jnp.int32, values.shape, 1)
    middle = HDIM // 2
    return jnp.where(
        lane % HDIM < middle,
        pltpu.roll(values, PAIR - middle, 1),
        pltpu.roll(values, middle, 1),
    )


def sigmoid(value):
    return 1.0 / (1.0 + jnp.exp(-value))


def first_of_pair(shape):
    return lax.broadcasted_iota(jnp.int32, shape, 1) < HDIM


def pair_keep(values, head):
    left = first_of_pair(values.shape)
    return jnp.where(left if head == 0 else ~left, values, jnp.zeros_like(values))


def allowed(rows, length):
    query = lax.broadcasted_iota(jnp.int32, (rows, rows), 0)
    key = lax.broadcasted_iota(jnp.int32, (rows, rows), 1)
    return (key <= query) & (key < length)


def attention_forward(micro, current, weights, gains, lengths, tables, order):
    query_key, rest = weights
    rows, width = current[0].shape
    parts = len(current)

    def body(*refs):
        length = refs[parts][micro, 0]
        wqk, rest_ref, gain, cosine, sine = refs[parts + 1 : parts + 6]
        hidden_out, normed_out, qk_out, v_out, mix_out, after_out, ffn_out = refs[parts + 6 :]
        hidden = refs[0][...].astype(F32)
        for ref in refs[1:parts]:
            hidden = hidden + ref[...].astype(F32)
        hidden_out[...] = hidden
        normed = low(hidden * rms_scale(hidden) * gain[0:1, :])
        normed_out[...] = normed
        projected = matmul(normed, wqk[...])
        values = low(matmul(normed, rest_ref[:, :width]))
        v_out[...] = values
        mask = allowed(rows, length)
        left = first_of_pair((rows, PAIR))
        for pair in range(width // PAIR):
            lanes = slice(pair * PAIR, (pair + 1) * PAIR)
            query = projected[:, lanes]
            query = low(query * cosine[...] + half_turn(query) * sine[...])
            key = projected[:, width + pair * PAIR : width + (pair + 1) * PAIR]
            key = low(key * cosine[...] + half_turn(key) * sine[...])
            qk_out[:, lanes] = query
            qk_out[:, width + pair * PAIR : width + (pair + 1) * PAIR] = key
            value = values[:, lanes]
            mixed = []
            for head in range(2):
                scores = contract_last(pair_keep(query, head), key) * SCALE
                scores = jnp.where(mask, scores, -1e30)
                exponent = jnp.exp(scores - jnp.max(scores, axis=-1, keepdims=True))
                probability = exponent / jnp.sum(exponent, axis=-1, keepdims=True)
                mixed.append(matmul(low(probability), value))
            mix_out[:, lanes] = low(jnp.where(left, mixed[0], mixed[1]))
        after_attn = hidden + matmul(mix_out[...], rest_ref[:, width : 2 * width])
        after_out[...] = after_attn
        ffn_out[...] = low(after_attn * rms_scale(after_attn) * gain[1:2, :])

    outs = [
        ((rows, width), F32),
        ((rows, width), BF16),
        ((rows, 2 * width), BF16),
        ((rows, width), BF16),
        ((rows, width), BF16),
        ((rows, width), F32),
        ((rows, width), BF16),
    ]
    return run(
        body,
        outs,
        [*current, scalars(lengths), query_key, rest, gains, *tables],
        order,
        flops=rows * width * width * 8,
    )


def attention_backward(micro, grad_out, parts, record, weights, gains, lengths, tables, order):
    query_key, rest = weights
    hidden, qk, values, after_attn = record
    rows, width = hidden.shape
    count = len(parts)

    def body(*refs):
        grad_ref = refs[0]
        length = refs[count + 1][micro, 0]
        hidden_ref, qk_ref, v_ref, after_ref, wqk, rest_ref, gain, cosine, sine = refs[
            count + 2 : count + 11
        ]
        grad_hidden, grad_low, attn_out, gqk_out, gv_out, gain_out = refs[count + 11 :]
        grad_ffn = refs[1][...].astype(F32)
        for ref in refs[2 : count + 1]:
            grad_ffn = grad_ffn + ref[...].astype(F32)
        back, gain_ffn = rms_back(after_ref[...], gain[1:2, :], grad_ffn)
        grad_after = grad_ref[...] + back
        grad_attn = low(grad_after)
        attn_out[...] = grad_attn
        grad_mix = low(contract_last(grad_attn, rest_ref[:, width : 2 * width]))
        mask = allowed(rows, length)
        left = first_of_pair((rows, PAIR))
        for pair in range(width // PAIR):
            lanes = slice(pair * PAIR, (pair + 1) * PAIR)
            far = slice(width + pair * PAIR, width + (pair + 1) * PAIR)
            query, key, value = (qk_ref[:, lanes], qk_ref[:, far], v_ref[:, lanes])
            grad = grad_mix[:, lanes]
            grad_v, grad_q, grad_k = ([], [], [])
            for head in range(2):
                scores = contract_last(pair_keep(query, head), key) * SCALE
                scores = jnp.where(mask, scores, -1e30)
                exponent = jnp.exp(scores - jnp.max(scores, axis=-1, keepdims=True))
                probability = exponent / jnp.sum(exponent, axis=-1, keepdims=True)
                grad_prob = contract_last(pair_keep(grad, head), value)
                grad_v.append(contract_first(low(probability), grad))
                inner = jnp.sum(probability * grad_prob, axis=-1, keepdims=True)
                grad_scores = low(probability * (grad_prob - inner))
                grad_q.append(matmul(grad_scores, key))
                grad_k.append(contract_first(grad_scores, query))
            grad_v = jnp.where(left, grad_v[0], grad_v[1])
            grad_q = jnp.where(left, grad_q[0], grad_q[1]) * SCALE
            grad_k = jnp.where(left, grad_k[0], grad_k[1]) * SCALE
            gv_out[:, lanes] = low(grad_v)
            gqk_out[:, lanes] = low(grad_q * cosine[...] - half_turn(grad_q) * sine[...])
            gqk_out[:, far] = low(grad_k * cosine[...] - half_turn(grad_k) * sine[...])
        grad_normed = contract_last(gqk_out[...], wqk[...]) + contract_last(
            gv_out[...], rest_ref[:, :width]
        )
        back, gain_attn = rms_back(hidden_ref[...], gain[0:1, :], grad_normed)
        total = grad_after + back
        grad_hidden[...] = total
        grad_low[...] = low(total)
        gain_out[...] = jnp.concatenate(
            [gain_attn, gain_ffn, jnp.zeros((6, width), F32)], axis=0
        )

    outs = [
        ((rows, width), F32),
        ((rows, width), BF16),
        ((rows, width), BF16),
        ((rows, 2 * width), BF16),
        ((rows, width), BF16),
        ((8, width), F32),
    ]
    return run(
        body,
        outs,
        [grad_out, *parts, scalars(lengths), hidden, qk, values, after_attn, query_key, rest, gains,
         *tables],
        order,
        flops=rows * width * width * 8,
    )


def fill_line(blocks, line_ref):
    rows = blocks[0].shape[0]
    for index, ref in enumerate(blocks):
        line_ref[index * rows : (index + 1) * rows, :] = ref[...]


def dispatch(blocks, place_row, gates_row, buffer_rows, order):
    count = len(blocks)
    rows, width = blocks[0].shape
    chunk = math.gcd(buffer_rows, 288)

    def body(*refs):
        place = refs[count]
        gates = refs[count + 1] if gates_row is not None else None
        line_ref, out_ref = refs[-2:]
        fill_line(refs[:count], line_ref)
        first, second = (place[0:1, :], place[1:2, :])
        if gates is None:
            first_gate, second_gate = (1.0, 1.0)
        else:
            first_gate, second_gate = (gates[0:1, :], gates[1:2, :])

        def step(index, carry):
            start = pl.multiple_of(index * chunk, 16)
            row = lax.broadcasted_iota(jnp.int32, (chunk, count * rows), 0) + index * chunk
            mixing = jnp.where(row == first, first_gate, 0.0)
            mixing = low(jnp.where(row == second, second_gate, mixing))
            out_ref[pl.ds(start, chunk), :] = low(matmul(mixing, line_ref[...]))
            return carry

        lax.fori_loop(0, buffer_rows // chunk, step, 0)

    extra = [] if gates_row is None else [gates_row]
    return run(
        body,
        [((count * rows, width), BF16), ((buffer_rows, width), BF16)],
        [*blocks, place_row, *extra],
        order,
        flops=2 * buffer_rows * count * rows * width,
    )


def routing_of(logits, columns, expert_count):
    lane = lax.broadcasted_iota(jnp.int32, logits.shape, 1)
    logits = jnp.where(lane < expert_count, logits, -1e30)
    exponent = jnp.exp(logits - jnp.max(logits, axis=-1, keepdims=True))
    probability = exponent / jnp.sum(exponent, axis=-1, keepdims=True)
    first = lane == columns[:, 2:3]
    second = lane == columns[:, 3:4]
    p_first = jnp.sum(jnp.where(first, probability, 0.0), axis=-1, keepdims=True)
    p_second = jnp.sum(jnp.where(second, probability, 0.0), axis=-1, keepdims=True)
    total = p_first + p_second
    return (probability, first, second, p_first / total, p_second / total, total)


def shared_forward(line_rows, shared, rest, columns, expert_count, order):
    gate_up, down = shared
    rows, width = line_rows.shape
    hidden_count = down.shape[0]

    def body(x_ref, gate_up_ref, down_ref, rest_ref, col_ref, out_ref, gates_ref, gates_row_ref):
        logits = matmul(x_ref[...], rest_ref[:, 2 * width :])
        _, _, _, gate_first, gate_second, _ = routing_of(logits, col_ref[...], expert_count)
        lane = lax.broadcasted_iota(jnp.int32, (rows, 128), 1)
        gates = jnp.where(lane == 0, gate_first, jnp.where(lane == 1, gate_second, 0.0))
        gates_ref[...] = gates
        gates_row_ref[...] = gates.T[:8]
        both = matmul(x_ref[...], gate_up_ref[...])
        gate_part = both[:, :hidden_count]
        hidden = low(gate_part * sigmoid(gate_part) * both[:, hidden_count:])
        out_ref[...] = matmul(hidden, down_ref[...])

    return run(
        body,
        [((rows, width), F32), ((rows, 128), F32), ((8, rows), F32)],
        [line_rows, gate_up, down, rest, columns],
        order,
        flops=6 * rows * width * hidden_count,
    )


def expert_forward(arrived, weights, order):
    rows, width = arrived.shape
    chunk = math.gcd(rows, 288)

    def body(x_ref, gate_ref, up_ref, down_ref, out_ref):
        def step(index, carry):
            place = pl.ds(pl.multiple_of(index * chunk, 16), chunk)
            x = x_ref[place, :]
            gate_part = matmul(x, gate_ref[...])
            up_part = matmul(x, up_ref[...])
            hidden = low(gate_part * sigmoid(gate_part) * up_part)
            out_ref[place, :] = low(matmul(hidden, down_ref[...]))
            return carry

        lax.fori_loop(0, rows // chunk, step, 0)

    return run(
        body, [((rows, width), BF16)], [arrived, *weights], order, flops=6 * rows * width * 512
    )[0]


def picks(columns, buffer_rows, first_gate, second_gate):
    lane = lax.broadcasted_iota(jnp.int32, (columns.shape[0], buffer_rows), 1)
    mixing = jnp.where(lane == columns[:, 0:1], first_gate, 0.0)
    return jnp.where(lane == columns[:, 1:2], second_gate, mixing)


def combine(returned, columns, gates, addend, blocks, order):
    buffer_rows, width = returned.shape
    tokens = addend.shape[0]
    rows = tokens // blocks

    def body(*refs):
        back_ref, col_ref, add_ref = refs[:3]
        outs = refs[-blocks:]
        step = math.gcd(tokens, 2 * rows)
        for start in range(0, tokens, step):
            place = slice(start, start + step)
            if gates is None:
                mixing = picks(col_ref[place, :], buffer_rows, 1.0, 1.0)
            else:
                gate_ref = refs[3]
                mixing = picks(
                    col_ref[place, :], buffer_rows, gate_ref[place, 0:1], gate_ref[place, 1:2]
                )
            total = matmul(low(mixing), back_ref[...]) + add_ref[place, :]
            for inside in range(step // rows):
                out = outs[start // rows + inside]
                out[...] = total[inside * rows : (inside + 1) * rows].astype(out.dtype)

    outs = [((rows, width), F32)] + [((rows, width), BF16)] * (blocks - 1)
    extra = [] if gates is None else [gates]
    return run(
        body,
        outs,
        [returned, columns, addend, *extra],
        order,
        flops=2 * buffer_rows * tokens * width,
    )


def shared_backward(grad_line, line_rows, shared, rest, returned, columns, expert_count, order):
    gate_up, down = shared
    rows, width = line_rows.shape
    hidden_count = down.shape[0]
    buffer_rows = returned.shape[0]

    def body(
        g_ref, x_ref, gate_up_ref, down_ref, rest_ref, back_ref, col_ref,
        out_ref, grads_ref, hidden_ref, logit_ref,
    ):
        x = x_ref[...]
        grad = g_ref[...]
        both = matmul(x, gate_up_ref[...])
        gate_part, up_part = (both[:, :hidden_count], both[:, hidden_count:])
        sigma = sigmoid(gate_part)
        silu = gate_part * sigma
        hidden_ref[...] = low(silu * up_part)
        grad_hidden = contract_last(grad, down_ref[...])
        grads_ref[:, :hidden_count] = low(
            grad_hidden * up_part * sigma * (1.0 + gate_part * (1.0 - sigma))
        )
        grads_ref[:, hidden_count:] = low(grad_hidden * silu)
        total = contract_last(grads_ref[...], gate_up_ref[...])
        router = rest_ref[:, 2 * width :]
        logits = matmul(x, router)
        probability, first, second, gate_first, gate_second, total_p = routing_of(
            logits, col_ref[...], expert_count
        )
        products = contract_last(grad, back_ref[...])
        lane = lax.broadcasted_iota(jnp.int32, (rows, buffer_rows), 1)
        grad_first = jnp.sum(
            jnp.where(lane == col_ref[:, 0:1], products, 0.0), axis=-1, keepdims=True
        )
        grad_second = jnp.sum(
            jnp.where(lane == col_ref[:, 1:2], products, 0.0), axis=-1, keepdims=True
        )
        mean = gate_first * grad_first + gate_second * grad_second
        grad_logits = jnp.where(first, gate_first * (grad_first - mean), 0.0)
        grad_logits = low(jnp.where(second, gate_second * (grad_second - mean), grad_logits))
        logit_ref[...] = grad_logits
        out_ref[...] = total + contract_last(grad_logits, router)

    outs = [
        ((rows, width), F32),
        ((rows, 2 * hidden_count), BF16),
        ((rows, hidden_count), BF16),
        ((rows, 128), BF16),
    ]
    return run(
        body,
        outs,
        [grad_line, line_rows, gate_up, down, rest, returned, columns],
        order,
        flops=2 * rows * width * (5 * hidden_count + buffer_rows),
    )


def expert_backward(grad_in, arrived, weights, order):
    rows, width = arrived.shape
    hidden_count = weights[2][0].shape[-2]
    chunk = math.gcd(rows, 288)

    def body(g_ref, x_ref, gate_ref, up_ref, down_ref, out_ref, grads_ref, hidden_ref):
        def step(index, carry):
            place = pl.ds(pl.multiple_of(index * chunk, 16), chunk)
            x = x_ref[place, :]
            gate_part = matmul(x, gate_ref[...])
            up_part = matmul(x, up_ref[...])
            sigma = sigmoid(gate_part)
            silu = gate_part * sigma
            hidden_ref[place, :] = low(silu * up_part)
            grad_hidden = contract_last(g_ref[place, :], down_ref[...])
            grad_gate = low(grad_hidden * up_part * sigma * (1.0 + gate_part * (1.0 - sigma)))
            grad_up = low(grad_hidden * silu)
            grads_ref[place, :hidden_count] = grad_gate
            grads_ref[place, hidden_count:] = grad_up
            out_ref[place, :] = low(
                contract_last(grad_gate, gate_ref[...]) + contract_last(grad_up, up_ref[...])
            )
            return carry

        lax.fori_loop(0, rows // chunk, step, 0)

    return run(
        body,
        [((rows, width), BF16), ((rows, 2 * hidden_count), BF16), ((rows, hidden_count), BF16)],
        [grad_in, arrived, *weights],
        order,
        flops=12 * rows * width * hidden_count,
    )


def expert_weight_grads(layer, layers, pairs, previous, order):
    count = len(pairs)
    rows, width = pairs[0][0].shape
    hidden_count = pairs[0][2].shape[1]

    def body(*refs):
        gate_out, up_out, down_out = refs[-3:]
        tile = math.gcd(width, 256)
        for start in range(0, width, tile):
            place = slice(start, start + tile)
            total = 0.0
            for micro in range(count):
                x_ref, grads_ref = refs[micro * 4 : micro * 4 + 2]
                total = total + contract_first(x_ref[:, place], grads_ref[...])
            gate_out[place, :] = total[:, :hidden_count]
            up_out[place, :] = total[:, hidden_count:]
        tile = math.gcd(hidden_count, 256)
        for start in range(0, hidden_count, tile):
            place = slice(start, start + tile)
            total = 0.0
            for micro in range(count):
                hidden_ref, in_ref = refs[micro * 4 + 2 : micro * 4 + 4]
                total = total + contract_first(hidden_ref[:, place], in_ref[...])
            down_out[place, :] = total

    shapes = [
        (layers, 1, width, hidden_count),
        (layers, 1, width, hidden_count),
        (layers, 1, hidden_count, width),
    ]
    operands = [array for pair in pairs for array in pair]
    specs = [pl.BlockSpec(memory_space=pltpu.VMEM)] * len(operands)
    anywhere = pl.BlockSpec(memory_space=pl.ANY)
    order = [jax.tree.leaves(item)[0] for item in order]
    old = [] if previous is None else list(previous)
    place = (layer, 0, 0, 0)
    total_flops = count * rows * width * hidden_count * 6

    def kernel(*refs):
        body(*refs[: len(operands)], *refs[-3:])

    return pl.pallas_call(
        kernel,
        out_shape=[jax.ShapeDtypeStruct(shape, F32) for shape in shapes],
        in_specs=specs + [anywhere] * (len(old) + len(order)),
        out_specs=[
            one_block((None, None) + shape[2:], place) for shape in shapes
        ],
        grid=(1,),
        input_output_aliases={len(operands) + index: index for index in range(len(old))},
        compiler_params=pltpu.CompilerParams(vmem_limit_bytes=48 * 1024 * 1024),
        cost_estimate=pl.CostEstimate(
            flops=total_flops, bytes_accessed=20 << 20, transcendentals=0
        ),
    )(*operands, *old, *order)


def shared_weight_grads(pairs, order):
    count = len(pairs)
    rows, width = pairs[0][0].shape
    hidden_count = pairs[0][2].shape[1]

    def body(*refs):
        both_out, down_out = refs[-2:]
        tile = math.gcd(width, 256)
        for start in range(0, width, tile):
            place = slice(start, start + tile)
            total = 0.0
            for micro in range(count):
                x_ref, grads_ref = refs[micro * 4 : micro * 4 + 2]
                total = total + contract_first(x_ref[:, place], grads_ref[...])
            both_out[place, :] = low(total)
        tile = math.gcd(hidden_count, 256)
        for start in range(0, hidden_count, tile):
            place = slice(start, start + tile)
            total = 0.0
            for micro in range(count):
                hidden_ref, in_ref = refs[micro * 4 + 2 : micro * 4 + 4]
                total = total + contract_first(hidden_ref[:, place], in_ref[...])
            down_out[place, :] = low(total)

    return run(
        body,
        [((width, 2 * hidden_count), BF16), ((hidden_count, width), BF16)],
        [array for pair in pairs for array in pair],
        order,
        flops=count * rows * width * hidden_count * 6,
    )


def attention_weight_grads(members, expert_count, order):
    each = len(members[0])
    count = len(members)
    width = members[0][0].shape[1]

    def body(*refs):
        qk_out, rest_out = refs[-2:]
        shape = (8, 128)
        row = lax.broadcasted_iota(jnp.int32, shape, 0)
        lane = lax.broadcasted_iota(jnp.int32, shape, 1)
        chosen = jnp.where((lane == expert_count + row) & (row < 2), 1.0, 0.0)
        tile = math.gcd(width, 256)
        for start in range(0, width, tile):
            place = slice(start, start + tile)
            qk, value, out, small = (0.0, 0.0, 0.0, 0.0)
            for micro in range(count):
                normed, mix, gqk, gv, ga, line, glogit, gains = refs[
                    micro * each : (micro + 1) * each
                ]
                qk = qk + contract_first(normed[:, place], gqk[...])
                value = value + contract_first(normed[:, place], gv[...])
                out = out + contract_first(mix[:, place], ga[...])
                small = small + contract_first(line[:, place], glogit[...])
                small = small + contract_first(gains[:, place], chosen)
            qk_out[place, :] = low(qk)
            rest_out[place, :width] = low(value)
            rest_out[place, width : 2 * width] = low(out)
            rest_out[place, 2 * width :] = low(small)

    return run(
        body,
        [((width, 2 * width), BF16), ((width, 2 * width + 128), BF16)],
        [array for member in members for array in member],
        order,
        flops=count * 128 * width * width * 8,
    )


def destinations(routes, expert_count, capacity, line_size):
    layers, micro, rows, top = routes.shape
    flat = routes.reshape(layers, micro, rows * top)
    matches = low(flat[..., None] == jnp.arange(expert_count))
    places = jnp.arange(rows * top)
    earlier = low(places[None, :] < places[:, None])
    before = jnp.einsum("pq,lmqe->lmpe", earlier, matches, preferred_element_type=F32)
    index = jnp.sum(before * matches.astype(F32), axis=-1).astype(jnp.int32)
    place = flat * (capacity * line_size) + index
    return place.reshape(layers, micro, rows, top)


class Clock:
    def __init__(self):
        self.last = ()

    def order(self):
        return self.last

    def done(self, result):
        self.last = (result,)
        return result

    def tie(self, value):
        return after(value, *self.last) if self.last else value


def on_device(
    tokens,
    lengths,
    routes,
    cotangent,
    attn_gain,
    qkv_weight,
    out_weight,
    ffn_gain,
    router_weight,
    shared_gate,
    shared_up,
    shared_down,
    expert_gate,
    expert_up,
    expert_down,
):
    line_size = lax.axis_size(LINE)
    dp_size = lax.axis_size(DP)
    expert_count = dp_size
    capacity = 9 * SLOT // (4 * expert_count)
    block_rows = capacity * line_size
    buffer_rows = expert_count * block_rows
    width = tokens.shape[-1]
    rows_owned = qkv_weight.shape[1]
    hidden_owned = shared_down.shape[1]
    tables = rope_tables(SLOT)
    sizes = [lax.axis_size(axis) for axis in ALL]
    small_cols = expert_count + 2
    assert small_cols <= 128
    clock = Clock()

    attention_weights = [None] * LAYERS
    shared_weights = [None] * LAYERS
    gain_rows = [None] * LAYERS
    expert_weights = [
        tuple(layer_block(weight, layer) for weight in (expert_gate, expert_up, expert_down))
        for layer in range(LAYERS)
    ]

    def gather_attention(layer):
        small = jnp.concatenate(
            [router_weight[layer], attn_gain[layer][:, None], ffn_gain[layer][:, None]], axis=1
        )
        small = jnp.pad(small, ((0, 0), (0, 128 - small_cols)))
        shard = jnp.concatenate([qkv_weight[layer], out_weight[layer], small], axis=1)
        shard = clock.tie(shard)
        others = send_axis(shard, LINE)
        yield
        shard, others = clock.tie((shard, others))
        line = order_axis(shard, others, LINE, 0)
        left, right = (line[..., : 2 * width], line[..., 2 * width :])
        others = (send_axis(left, "x"), send_axis(right, "y"))
        yield
        left, right, others = clock.tie((left, right, others))
        left = order_axis(left, others[0], "x", 0)
        right = order_axis(right, others[1], "y", 0)
        others = (send_axis(left, "y"), send_axis(right, "x"))
        yield
        left, right, others = clock.tie((left, right, others))
        left = order_axis(left, others[0], "y", 0)
        right = order_axis(right, others[1], "x", 1)
        others = (send_axis(left, "core"), send_axis(right, "core"))
        yield
        left, right, others = clock.tie((left, right, others))
        left = order_axis(left, others[0], "core", 2).reshape(width, 2 * width)
        right = order_axis(right, others[1], "core", 2).reshape(width, -1)
        attention_weights[layer] = (left, right)
        gains = right[:, 2 * width + expert_count : 2 * width + small_cols].T.astype(F32)
        gain_rows[layer] = jnp.pad(gains, ((0, 6), (0, 0)))
        yield

    def gather_shared(layer):
        gate_shard, up_shard, down = clock.tie(
            (shared_gate[layer], shared_up[layer], shared_down[layer])
        )
        both = jnp.stack(
            [
                weight.reshape(rows_owned, dp_size, line_size, hidden_owned)
                for weight in (gate_shard, up_shard)
            ]
        )
        blocks = jnp.transpose(both, (3, 1, 0, 2, 4)).reshape(line_size, rows_owned, -1)
        me = lax.axis_index(LINE)
        pieces = [
            lax.dynamic_index_in_dim(blocks, (me + step) % line_size, 0, keepdims=False)
            for step in range(line_size)
        ]
        others = [shift(pieces[step], LINE, step) for step in range(1, line_size)]
        down_others = send_axis(down, "y")
        yield
        pieces, others, down, down_others = clock.tie((pieces[0], others, down, down_others))
        both = order_axis(pieces, others, LINE, 0)
        down = order_axis(down, down_others, "y", 0)
        others, down_others = (send_axis(both, "x"), send_axis(down, "x"))
        yield
        both, others, down, down_others = clock.tie((both, others, down, down_others))
        both = order_axis(both, others, "x", 0)
        down = order_axis(down, down_others, "x", 1)
        others, down_others = (send_axis(both, "y"), send_axis(down, "core"))
        yield
        both, others, down, down_others = clock.tie((both, others, down, down_others))
        both = order_axis(both, others, "y", 0)
        down = order_axis(down, down_others, "core", 2)
        others = send_axis(both, "core")
        yield
        both, others = clock.tie((both, others))
        both = order_axis(both, others, "core", 2)
        shared_weights[layer] = (both.reshape(width, -1), down.reshape(-1, width))
        yield

    def part(value, axis, place, step):
        index = (lax.axis_index(axis) + step) % lax.axis_size(axis)
        return lax.dynamic_index_in_dim(value, index, place, keepdims=False)

    def send_parts(value, axis, place):
        return [
            shift(part(value, axis, place, step), axis, step)
            for step in range(1, lax.axis_size(axis))
        ]

    def add_parts(value, others, axis, place, kind=BF16):
        total = part(value, axis, place, 0).astype(F32)
        for other in others:
            total = total + other.astype(F32)
        return total.astype(kind)

    owned = [{} for _ in range(LAYERS)]

    def scatter_attention(layer, left, right):
        left = left.reshape(*sizes, rows_owned, -1)
        right = right.reshape(*sizes, rows_owned, -1)
        for axes, places in ((("core", "core"), (2, 2)), (("x", "y"), (1, 0)), (("y", "x"), (0, 0))):
            others = (
                send_parts(left, axes[0], places[0]),
                send_parts(right, axes[1], places[1]),
            )
            yield
            left, right, others = clock.tie((left, right, others))
            left = add_parts(left, others[0], axes[0], places[0])
            right = add_parts(right, others[1], axes[1], places[1])
        both = jnp.concatenate([left, right], axis=-1)
        others = send_parts(both, LINE, 0)
        yield
        both, others = clock.tie((both, others))
        mine = add_parts(both, others, LINE, 0, F32)
        owned[layer]["qkv"] = mine[:, : 3 * width]
        owned[layer]["out"] = mine[:, 3 * width : 4 * width]
        small = mine[:, 4 * width :]
        owned[layer]["router"] = small[:, :expert_count]
        owned[layer]["attn_gain"] = small[:, expert_count]
        owned[layer]["ffn_gain"] = small[:, expert_count + 1]
        yield

    def scatter_shared(layer, both, down):
        both = both.reshape(*sizes, rows_owned, -1)
        down = down.reshape(*sizes[:3], hidden_owned, width)
        kinds = (BF16, BF16, F32)
        stages = ((("core", "core"), (2, 2)), (("x", "y"), (1, 0)), (("y", "x"), (0, 0)))
        for (axes, places), kind in zip(stages, kinds):
            others = (
                send_parts(both, axes[0], places[0]),
                send_parts(down, axes[1], places[1]),
            )
            yield
            both, down, others = clock.tie((both, down, others))
            both = add_parts(both, others[0], axes[0], places[0])
            down = add_parts(down, others[1], axes[1], places[1], kind)
        owned[layer]["down"] = down
        mine = part(both, LINE, 0, 0)
        others = send_parts(both, LINE, 0)
        yield
        mine, others = clock.tie((mine, others))
        both = order_axis(mine, others, LINE, 0)
        both = both.reshape(line_size, rows_owned, 2, dp_size, hidden_owned)
        both = jnp.transpose(both, (2, 1, 3, 0, 4)).reshape(2, rows_owned, -1).astype(F32)
        owned[layer]["gate"] = both[0]
        owned[layer]["up"] = both[1]
        yield

    background = []

    def advance(count=1):
        for stages in background[:count]:
            if next(stages, "end") == "end":
                background.remove(stages)

    def finish():
        while background:
            advance(len(background))

    own_routes = routes[:, :, 0]
    place = destinations(own_routes, expert_count, capacity, line_size)
    routing = line_blocks(jnp.concatenate([place, own_routes], axis=-1))
    offsets = jnp.array([1, 1, 0, 0], jnp.int32) * capacity
    columns_all = jnp.concatenate(
        [block + step * offsets for step, block in enumerate(routing)], axis=2
    )
    rows_all = jnp.swapaxes(columns_all, 2, 3)

    def columns(layer, micro):
        return columns_all[layer, micro]

    def place_row(layer, micro):
        return rows_all[layer, micro]

    micros = range(MICRO)
    state = {}

    def attend(layer, micro, current):
        result = clock.done(
            attention_forward(
                micro, current, attention_weights[layer], gain_rows[layer], lengths, tables,
                clock.order(),
            )
        )
        state[layer, micro, "attend"] = result
        state[layer, micro, "line"] = line_blocks(result[6])

    def send_rows(layer, micro):
        line, outbound = clock.done(
            dispatch(
                state[layer, micro, "line"], place_row(layer, micro), None, buffer_rows,
                clock.order(),
            )
        )
        state[layer, micro, "rows"] = line
        state[layer, micro, "arrived"] = swap_experts(outbound, expert_count)

    def share(layer, micro):
        state[layer, micro, "shared"] = clock.done(
            shared_forward(
                state[layer, micro, "rows"], shared_weights[layer], attention_weights[layer][1],
                columns(layer, micro), expert_count, clock.order(),
            )
        )

    def expert(layer, micro):
        produced = clock.done(
            expert_forward(state[layer, micro, "arrived"], expert_weights[layer], clock.order())
        )
        state[layer, micro, "returned"] = swap_experts(produced, expert_count)

    def gather_picks(layer, micro):
        shared_out, gates, _ = state[layer, micro, "shared"]
        blocks = clock.done(
            combine(
                state[layer, micro, "returned"], columns(layer, micro), gates, shared_out,
                line_size, clock.order(),
            )
        )
        state[layer, micro, "result"] = [state[layer, micro, "attend"][5], *line_return(blocks)]

    def gather_grads(layer, micro, grad):
        state[layer, micro, "grad_line"] = line_blocks(grad)

    def send_grads(layer, micro):
        line, outbound = clock.done(
            dispatch(
                state[layer, micro, "grad_line"], place_row(layer, micro),
                state[layer, micro, "shared"][2], buffer_rows, clock.order(),
            )
        )
        state[layer, micro, "grad_rows"] = line
        state[layer, micro, "grad_in"] = swap_experts(outbound, expert_count)

    def share_back(layer, micro):
        state[layer, micro, "shared_back"] = clock.done(
            shared_backward(
                state[layer, micro, "grad_rows"], state[layer, micro, "rows"],
                shared_weights[layer], attention_weights[layer][1],
                state[layer, micro, "returned"], columns(layer, micro), expert_count,
                clock.order(),
            )
        )

    def expert_back(layer, micro):
        rows_back, grads, hidden = clock.done(
            expert_backward(
                state[layer, micro, "grad_in"], state[layer, micro, "arrived"],
                expert_weights[layer], clock.order(),
            )
        )
        state[layer, micro, "back"] = swap_experts(rows_back, expert_count)
        state[layer, micro, "expert_pair"] = (
            state[layer, micro, "arrived"], grads, hidden, state[layer, micro, "grad_in"],
        )

    expert_grads = [None]

    def expert_weights_back(layer):
        pairs = [state[layer, micro, "expert_pair"] for micro in micros]
        expert_grads[0] = clock.done(
            expert_weight_grads(layer, LAYERS, pairs, expert_grads[0], clock.order())
        )

    def gather_back(layer, micro):
        blocks = clock.done(
            combine(
                state[layer, micro, "back"], columns(layer, micro), None,
                state[layer, micro, "shared_back"][0], line_size, clock.order(),
            )
        )
        state[layer, micro, "grad_ffn"] = line_return(blocks)

    def shared_weights_back(layer):
        pairs = [
            (
                state[layer, micro, "rows"],
                state[layer, micro, "shared_back"][1],
                state[layer, micro, "shared_back"][2],
                state[layer, micro, "grad_rows"],
            )
            for micro in micros
        ]
        both, down = clock.done(shared_weight_grads(pairs, clock.order()))
        background.append(scatter_shared(layer, both, down))

    def attend_back(layer, micro, grad):
        hidden, _, qk, values, _, after_attn, _ = state[layer, micro, "attend"]
        result = clock.done(
            attention_backward(
                micro, grad, state[layer, micro, "grad_ffn"], (hidden, qk, values, after_attn),
                attention_weights[layer], gain_rows[layer], lengths, tables, clock.order(),
            )
        )
        state[layer, micro, "attend_back"] = result
        return result

    def attention_weights_back(layer):
        members = []
        for micro in micros:
            front = state[layer, micro, "attend"]
            back = state[layer, micro, "attend_back"]
            members.append(
                (
                    front[1], front[4], back[3], back[4], back[2],
                    state[layer, micro, "rows"], state[layer, micro, "shared_back"][3], back[5],
                )
            )
        left, right = clock.done(
            attention_weight_grads(members, expert_count, clock.order())
        )
        background.append(scatter_attention(layer, left, right))

    valid = [
        (jnp.arange(SLOT) < lengths[micro, 0]).astype(F32)[:, None] for micro in micros
    ]
    grads = [cotangent[micro, 0].astype(F32) * valid[micro] for micro in micros]
    low_grads = [low(grad) for grad in grads]
    for _ in gather_attention(0):
        pass
    currents = [[tokens[micro, 0]] for micro in micros]
    clock.done(attention_weights[0])
    background.append(gather_shared(0))
    last = LAYERS - 1
    for layer in range(LAYERS):
        advance()
        for micro in micros:
            attend(layer, micro, currents[micro])
            advance()
        for micro in micros:
            send_rows(layer, micro)
            advance()
        if layer == 0:
            low_grads = clock.tie(low_grads)
            for micro in micros:
                gather_grads(last, micro, low_grads[micro])
        finish()
        for micro in micros:
            share(layer, micro)
            if layer == last:
                send_grads(layer, micro)
        if layer == last:
            break
        background.append(gather_attention(layer + 1))
        advance()
        for micro in micros:
            expert(layer, micro)
            advance()
        for micro in micros:
            gather_picks(layer, micro)
            advance()
        finish()
        background.append(gather_shared(layer + 1))
        currents = [state[layer, micro, "result"] for micro in micros]

    outputs = []
    for layer in reversed(range(LAYERS)):
        if layer == last:
            for micro in micros:
                expert(layer, micro)
        else:
            for micro in micros:
                send_grads(layer, micro)
                advance(2)
            for micro in micros:
                share_back(layer, micro)
                advance(2)
        for micro in micros:
            expert_back(layer, micro)
            advance(2)
        if layer == last:
            for micro in micros:
                share_back(layer, micro)
        expert_weights_back(layer)
        advance(2)
        if layer == last:
            for micro in micros:
                gather_picks(layer, micro)
        for micro in micros:
            gather_back(layer, micro)
            advance(2)
        shared_weights_back(layer)
        advance(2)
        for micro in micros:
            result = attend_back(layer, micro, grads[micro])
            grads[micro] = result[0]
            if layer > 0:
                gather_grads(layer - 1, micro, result[1])
            advance(2)
        attention_weights_back(layer)
        advance(2)
        if layer == last:
            for micro in micros:
                total = state[layer, micro, "result"][0]
                for piece in state[layer, micro, "result"][1:]:
                    total = total + piece.astype(F32)
                outputs.append(total)
    finish()

    def stacked(name):
        return jnp.stack([owned[layer][name] for layer in range(LAYERS)])

    return (
        jnp.stack(outputs)[:, None],
        jnp.stack(grads)[:, None],
        stacked("attn_gain"),
        stacked("qkv"),
        stacked("out"),
        stacked("ffn_gain"),
        stacked("router"),
        stacked("gate"),
        stacked("up"),
        stacked("down"),
        *expert_grads[0],
    )


def solution(mesh):
    dp_size, line_size = mesh.devices.shape
    fine = Mesh(mesh.devices.reshape(dp_size // 4, 2, 2, line_size), ALL)
    rows_of = {
        2: P(None, ALL),
        3: P(None, ALL, None),
        4: P(None, ALL, None, None),
    }
    experts = (P(None, DP, None, LINE), P(None, DP, None, LINE), P(None, DP, LINE, None))
    rows_three = rows_of[3]
    weights = (
        rows_of[2], rows_three, rows_three, rows_of[2], rows_three, rows_three, rows_three,
        rows_three,
    )
    in_specs = (
        rows_of[4],
        rows_of[2],
        P(None, None, ALL, None, None),
        rows_of[4],
        *weights,
        *experts,
    )
    out_specs = (rows_of[4], rows_of[4], *weights, *experts)
    return jax.shard_map(
        on_device, mesh=fine, in_specs=in_specs, out_specs=out_specs, check_vma=False
    )
```
